512 devices in a mesh: fork: 32 (over z_hi, y, core), rep: 4 (over z_lo), tp: 4 (over x).
Axes of the slice: x: 4, y: 4, z: 16 (z_hi: 4, z_lo: 4; z = z_hi * 4 + z_lo), core: 2. Of those that a mesh axis runs over, the one named last changes fastest.
Arguments:
- prompt_hidden: bfloat16 [32, 32, 256, 5120], P('fork', None, 'rep', 'tp'), may hold values from -6 to 6
- lengths: int32 [32], replicated, may hold values from 1024 to 8192, as said below
- owner: int32 [32], replicated, may hold values from 0 to 127
- w_key: bfloat16 [5120, 512], P('tp', 'rep'), may hold values from -0.078125 to 0.078125
- w_value: bfloat16 [5120, 512], P('tp', 'rep'), may hold values from -0.078125 to 0.078125
- k_gain: float32 [128], replicated, may hold values from 0.9 to 1.5
- q_gain: float32 [128], replicated, may hold values from 0.9 to 1.5
- decode_query: bfloat16 [32, 16, 8, 4096], P('fork', 'rep', None, 'tp'), may hold values from -6 to 6
- decode_key: bfloat16 [32, 16, 8, 512], P('fork', 'rep', None, 'tp'), may hold values from -6 to 6
- decode_value: bfloat16 [32, 16, 8, 512], P('fork', 'rep', None, 'tp'), may hold values from -6 to 6
Outputs:
- attended: bfloat16 [32, 16, 8, 4096], P('fork', 'rep', None, 'tp')
The draws below stay inside these ranges and needn't reach their ends.
Inputs may be any that keep to these rules, and one draw needn't show every extreme that they name: `lengths`: some prompt has length exactly 8192.
All inputs are finite; a program needn't handle non-finite values.
Results may differ from the reference program's by a relative error of at most 0.03.
Values may be sent and summed in bfloat16 or wider, within the bound.
No kernel may reach another device: no remote copies, remote signals or barrier semaphores. Data moves between devices by JAX's collectives and lax.ppermute only.
A program may use at most 64 MiB of HBM per device.

```python
import math
import jax
import jax.numpy as jnp
from jax import lax

D = 5120
HD = 128
QPK = 8
STEPS = 8
PAGE_DEV = 64
SAMP_DEV = 4
PROMPTS = 32
PAGE = 256
LMAX = 8192
SAMP_GROUP = 16
KV_HEADS = 4
QH = 32
N_FORK = 32
N_REP = 4
N_TP = 4


def draw_lengths(key, part):
    key = jax.random.fold_in(key, 11)
    first_key, second_key = jax.random.split(key)
    values = jax.random.randint(first_key, (PROMPTS,), LMAX // 8, LMAX + 1)
    chosen = jax.random.randint(second_key, (), 0, PROMPTS)
    return jnp.where(jnp.arange(PROMPTS) == chosen, LMAX, values).astype(jnp.int32)


def plant(drawn, own_key, least, top_value):
    extent = drawn.shape
    place = [jax.random.randint(jax.random.fold_in(own_key, axis), (), 0, extent[axis]) for axis in range(len(extent))]
    drawn = drawn.at[tuple(place)].set(least)
    longest = extent.index(max(extent))
    place[longest] = (place[longest] + 1) % extent[longest]
    return drawn.at[tuple(place)].set(top_value)


def block_scale(rng, shape, cuts, least, largest):
    loudness, own = 1.0, jax.random.fold_in(rng, 6)
    for dim, shards_of in cuts:
        steps = jnp.exp(jax.random.uniform(jax.random.fold_in(own, dim), (shards_of,), jnp.float32, least / len(cuts), largest / len(cuts)))
        loudness = loudness * jnp.repeat(steps, shape[dim] // shards_of).reshape([-1 if axis == dim else 1 for axis in range(len(shape))])
    return loudness


def bell_draw(key, shape, scale, reach, pieces=(), kind=jnp.bfloat16):
    entries = scale * jax.random.normal(key, shape, jnp.float32)
    if pieces:
        entries = entries * block_scale(key, shape, pieces, -0.22, 0.18)
    return jnp.clip(entries, -reach, reach).astype(kind)


def setup_inputs(seed: int = 0) -> dict:
    key_list = jax.random.split(jax.random.key(seed), 11)
    return {
        "prompt_hidden": bell_draw(key_list[0], (N_FORK, PROMPTS, PAGE, D), 1.0, 6.0, ((0, 32), (2, 4), (3, 4))),
        "lengths": draw_lengths(jax.random.fold_in(key_list[10], 71), 0),
        "owner": plant(jax.random.randint(key_list[2], (PROMPTS,), 0, N_FORK * N_REP), jax.random.fold_in(key_list[2], 1), 0, (N_FORK * N_REP) - 1).astype(jnp.int32),
        "w_key": bell_draw(key_list[3], (D, KV_HEADS * HD), D ** -0.5, 0.078125, ((0, 4), (1, 4))),
        "w_value": bell_draw(key_list[4], (D, KV_HEADS * HD), D ** -0.5, 0.078125, ((0, 4), (1, 4))),
        "k_gain": jnp.clip(jnp.exp(jax.random.uniform(key_list[5], (HD,), jnp.float32, math.log(0.9), math.log(1.5))), 0.9, 1.5),
        "q_gain": jnp.clip(jnp.exp(jax.random.uniform(key_list[6], (HD,), jnp.float32, math.log(0.9), math.log(1.5))), 0.9, 1.5),
        "decode_query": bell_draw(key_list[7], (N_FORK, SAMP_GROUP, STEPS, QH * HD), 1.0, 6.0, ((0, 32), (1, 4), (3, 4))),
        "decode_key": bell_draw(key_list[8], (N_FORK, SAMP_GROUP, STEPS, KV_HEADS * HD), 1.0, 6.0, ((0, 32), (1, 4), (3, 4))),
        "decode_value": bell_draw(key_list[9], (N_FORK, SAMP_GROUP, STEPS, KV_HEADS * HD), 1.0, 6.0, ((0, 32), (1, 4), (3, 4))),
    }


def normed(vector, gain):
    return vector * lax.rsqrt(lax.optimization_barrier(jnp.mean(vector * vector, axis=-1, keepdims=True)) + 1e-06) * gain

def rotary(vector, position):
    half_dim = vector.shape[-1] // 2
    frequency = jnp.exp(jnp.arange(half_dim, dtype=jnp.float32) * (-2.0 * math.log(1000000.0) / vector.shape[-1]))
    angles = position[..., None] * frequency
    cos_table = jnp.cos(angles)
    sin_table = jnp.sin(angles)
    first_half = vector[..., :half_dim]
    second_half = vector[..., half_dim:]
    return jnp.concatenate([first_half * cos_table - second_half * sin_table, second_half * cos_table + first_half * sin_table], axis=-1)

def reference(prompt_hidden, lengths, owner, w_key, w_value, k_gain, q_gain, decode_query, decode_key, decode_value):
    page_len = PAGE_DEV * N_REP
    max_len = page_len * N_FORK
    width = D // N_TP
    block_total = N_FORK * N_REP
    sample_total = SAMP_DEV * N_REP
    weight_both = jnp.concatenate([w_key, w_value], axis=1).astype(jnp.float32).reshape(N_TP, width, 2 * N_TP * HD)
    scale = 1.0 / math.sqrt(HD)
    causal = jnp.arange(STEPS, dtype=jnp.int32)[None, :] <= jnp.arange(STEPS, dtype=jnp.int32)[:, None]

    def one_prompt(inputs):
        prompt, query_raw, new_key_raw, new_value = inputs
        length = lengths[prompt]
        sources = (owner[prompt] + jnp.arange(block_total, dtype=jnp.int32)) % block_total
        blocks = prompt_hidden[:, prompt].reshape(block_total, PAGE_DEV, D)[sources]
        feature = blocks.reshape(max_len, N_TP, width).astype(jnp.float32)
        partial_value = jnp.einsum('ltd,tdc->tlc', feature, weight_both).astype(jnp.bfloat16)
        summed = lax.optimization_barrier(jnp.sum(partial_value.astype(jnp.float32), axis=0))
        key_raw = summed[:, :N_TP * HD].reshape(max_len, N_TP, HD)
        prompt_value = summed[:, N_TP * HD:].reshape(max_len, N_TP, HD).astype(jnp.bfloat16)
        slots = jnp.arange(max_len, dtype=jnp.int32)
        prompt_key = rotary(normed(key_raw, k_gain), slots.astype(jnp.float32)[:, None]).astype(jnp.bfloat16)
        step_position = (length + jnp.arange(STEPS, dtype=jnp.int32)).astype(jnp.float32)
        query = query_raw.astype(jnp.float32).reshape(sample_total, STEPS, N_TP, QPK, HD)
        query = rotary(normed(query, q_gain), step_position[None, :, None, None]).astype(jnp.bfloat16)
        new_key = new_key_raw.astype(jnp.float32).reshape(sample_total, STEPS, N_TP, HD)
        new_key = rotary(normed(new_key, k_gain), step_position[None, :, None]).astype(jnp.bfloat16)
        values_new = new_value.reshape(sample_total, STEPS, N_TP, HD)
        old_scores = jnp.einsum('asgqd,lgd->asgql', query.astype(jnp.float32), prompt_key.astype(jnp.float32)) * scale
        old_exp = jnp.where(slots < length, jnp.exp(old_scores), 0.0)
        new_scores = jnp.einsum('asgqd,augd->asgqu', query.astype(jnp.float32), new_key.astype(jnp.float32)) * scale
        new_exp = jnp.where(causal[None, :, None, None, :], jnp.exp(new_scores), 0.0)
        total = lax.optimization_barrier(jnp.sum(old_exp, axis=-1, keepdims=True)) + lax.optimization_barrier(jnp.sum(new_exp, axis=-1, keepdims=True))
        old_weight = (old_exp / total).astype(jnp.bfloat16)
        new_weight = (new_exp / total).astype(jnp.bfloat16)
        result = jnp.einsum('asgql,lgd->asgqd', old_weight.astype(jnp.float32), prompt_value.astype(jnp.float32))
        result = result + jnp.einsum('asgqu,augd->asgqd', new_weight.astype(jnp.float32), values_new.astype(jnp.float32))
        return result.reshape(sample_total, STEPS, N_TP * QPK * HD).astype(jnp.bfloat16)
    return lax.map(one_prompt, (jnp.arange(N_FORK, dtype=jnp.int32), decode_query, decode_key, decode_value))
```

```python
import functools
import math

import jax
import jax.numpy as jnp
from jax import lax
from jax.experimental import pallas as pl
from jax.experimental.pallas import tpu as pltpu
from jax.sharding import Mesh, PartitionSpec as P

BF16 = jnp.bfloat16
F32 = jnp.float32
HEAD = 128
BLOCK = 64
DELTA = (3, 0, 2, 1)
Z_GROUP = ("zl", "y", "c")
Z_LINE = ("zh", "zl")
Z_CORE = ("zh", "c", "zl")
PAIRS = (
    ((0, 1), (1, 0), (2, 3), (3, 2)),
    ((0, 3), (3, 0), (1, 2), (2, 1)),
)


def shift_core(step0, step1):
    place = lambda z, c: (z % 16 // 4 * 2 + c) * 4 + z % 4
    return [(place(z, c), place(z + step, c)) for z in range(16) for c, step in enumerate((step0, step1))]


def home_routes():
    routes = [[] for _ in range(4)]
    for group in range(4):
        for place, delta in enumerate(DELTA):
            prompt_group = (group + delta) % 4
            for rep in range(4):
                routes[(rep + delta) % 4].append((group * 4 + place, prompt_group * 4 + rep))
    return routes


def params(mib=20):
    return pltpu.CompilerParams(vmem_limit_bytes=mib * 2**20)


def rms_scale(v):
    return v * lax.rsqrt(jnp.mean(v * v, axis=-1, keepdims=True) + 1e-06)


def turn(v, cos, sin):
    return v * cos + pltpu.roll(v, HEAD // 2, 1) * sin


def prep_kernel(dq, dk, dv, qg, kg, cos, sin, q_out, num_out, den_out):
    heads = dq.shape[1] // HEAD
    rows = dq.shape[0]
    cos, sin = cos[...], sin[...]
    for head in range(heads):
        v = dq[:, head * HEAD : (head + 1) * HEAD].astype(F32)
        q_out[head * rows : (head + 1) * rows, :] = turn(rms_scale(v) * qg[...], cos, sin).astype(BF16)
    key = turn(rms_scale(dk[...].astype(F32)) * kg[...], cos, sin).astype(BF16)
    scores = lax.dot_general(key, q_out[...], (((1,), (1,)), ((), ())), preferred_element_type=F32)
    k_row = lax.broadcasted_iota(jnp.int32, scores.shape, 0)
    q_col = lax.broadcasted_iota(jnp.int32, scores.shape, 1) & (rows - 1)
    seen = ((k_row >> 3) == (q_col >> 3)) & ((k_row & 7) <= (q_col & 7))
    weight = jnp.where(seen, jnp.exp(scores * (1.0 / math.sqrt(HEAD))), 0.0)
    den_out[...] = jnp.sum(weight, axis=0, keepdims=True)
    num_out[...] = lax.dot_general(
        dv[...].astype(F32).T.astype(BF16), weight.astype(BF16), (((1,), (0,)), ((), ())), preferred_element_type=F32
    )


def prep(dq, dk, dv, qg, kg, cos, sin):
    rows = dq.shape[0]
    n = dq.shape[1] // HEAD * rows
    return pl.pallas_call(
        prep_kernel,
        out_shape=(
            jax.ShapeDtypeStruct((n, HEAD), BF16),
            jax.ShapeDtypeStruct((HEAD, n), F32),
            jax.ShapeDtypeStruct((1, n), F32),
        ),
        compiler_params=params(),
        name="prep",
    )(dq, dk, dv, qg, kg, cos, sin)


def project_kernel(per_half, info, x, *rest):
    pieces, outs, (wbuf, sems) = rest[:4], rest[4:-2], rest[-2:]
    for j, piece in enumerate(pieces):
        pltpu.make_async_copy(piece, wbuf.at[j], sems.at[j]).start()
    for j, piece in enumerate(pieces):
        pltpu.make_async_copy(piece, wbuf.at[j], sems.at[j]).wait()
    for i, out in enumerate(outs):
        half = i // per_half
        w = jnp.concatenate([wbuf[info[4 + 2 * i]], wbuf[info[5 + 2 * i]]], axis=1)
        first = out.shape[0] - 2
        n = x.shape[1]
        for k in range(2):
            y = jnp.dot(x[info[2 * half + k]], w, preferred_element_type=F32).astype(BF16)
            out[first, k * n : (k + 1) * n, :] = y[:, :HEAD]
            out[first + 1, k * n : (k + 1) * n, :] = y[:, HEAD:]


def project(places, info, hidden, pieces):
    _, rows, width = hidden.shape
    outs = [jax.ShapeDtypeStruct((n, 2 * rows, HEAD), BF16) for n in places]
    vmem = pl.BlockSpec(memory_space=pltpu.VMEM)
    return pl.pallas_call(
        functools.partial(project_kernel, len(outs) // 2),
        in_specs=[pl.BlockSpec(memory_space=pltpu.SMEM), vmem] + [pl.BlockSpec(memory_space=pl.ANY)] * 4,
        out_specs=[vmem] * len(outs),
        out_shape=outs,
        scratch_shapes=[pltpu.VMEM((4, width, HEAD), BF16), pltpu.SemaphoreType.DMA((4,))],
        compiler_params=params(24),
        cost_estimate=pl.CostEstimate(
            flops=2 * 2 * rows * width * len(outs) * 2 * HEAD,
            bytes_accessed=4 * rows * (width * 2 + len(outs) * HEAD * 2),
            transcendentals=0,
        ),
        name="project",
    )(info, hidden, *pieces)


def pair_sum_kernel(keep, first, *rest):
    rest[-1][0] = (keep[0].astype(F32) + first[0].astype(F32)).astype(BF16)


def pair_sum(keep, first, *buffer):
    rows = keep.shape[1]
    last = [pl.BlockSpec((1, rows, HEAD), lambda i, at=a.shape[0] - 1: (at, 0, 0)) for a in (keep, first)]
    return pl.pallas_call(
        pair_sum_kernel,
        grid=(1,),
        in_specs=last + [pl.BlockSpec(memory_space=pl.ANY)] * len(buffer),
        out_specs=pl.BlockSpec((1, rows, HEAD), lambda i: (0, 0, 0)),
        out_shape=jax.ShapeDtypeStruct(buffer[0].shape if buffer else (1, rows, HEAD), BF16),
        input_output_aliases={2: 0} if buffer else {},
        compiler_params=params(),
        name="pair_sum",
    )(keep, first, *buffer)


def finish_kernel(is_key, ka, ra, sa, kb, rb, sb, gain, cos_b, sin_b, cos_i, sin_i, out):
    step = pl.program_id(0)

    def run(keep, first, second):
        total = keep[0].astype(F32) + first[0].astype(F32) + second[0].astype(F32)

        @pl.when(is_key[0] == 0)
        def _():
            out[...] = total.astype(BF16)

        @pl.when(is_key[0] == 1)
        def _():
            scaled = rms_scale(total) * gain[...]
            ci, si = cos_i[...], sin_i[...]
            for b in range(total.shape[0] // BLOCK):
                cb, sb_ = cos_b[b : b + 1, :], sin_b[b : b + 1, :]
                cos = cb * ci - sb_ * si
                sin = sb_ * ci + cb * si
                out[b * BLOCK : (b + 1) * BLOCK, :] = turn(scaled[b * BLOCK : (b + 1) * BLOCK, :], cos, sin).astype(BF16)

    @pl.when(step < 2)
    def _():
        run(ka, ra, sa)

    @pl.when(step >= 2)
    def _():
        run(kb, rb, sb)


def finish(is_key, parts, starts, extra):
    rows = parts[0].shape[1] // 2
    low = lambda i: jnp.minimum(i, 1)
    high = lambda i: jnp.maximum(i - 2, 0)
    specs = []
    for place in (low, high):
        for start in starts:
            specs.append(pl.BlockSpec((1, rows, HEAD), lambda i, k, place=place, start=start: (start, place(i), 0)))
    per = pl.BlockSpec((rows // BLOCK, HEAD), lambda i, k: (i, 0))
    whole = lambda a: pl.BlockSpec(a.shape, lambda i, k: (0, 0))
    specs += [whole(extra[0]), per, per, whole(extra[3]), whole(extra[4])]
    return pl.pallas_call(
        finish_kernel,
        grid_spec=pltpu.PrefetchScalarGridSpec(
            num_scalar_prefetch=1,
            grid=(4,),
            in_specs=specs,
            out_specs=pl.BlockSpec((rows, HEAD), lambda i, k: (i, 0)),
        ),
        out_shape=jax.ShapeDtypeStruct((4 * rows, HEAD), BF16),
        compiler_params=params(),
        name="finish",
    )(is_key, *parts, *extra)


def exp_scores(live, line, core, keys, queries):
    scores = lax.dot_general(keys, queries, (((1,), (1,)), ((), ())), preferred_element_type=F32)
    row = lax.broadcasted_iota(jnp.int32, (keys.shape[0], 1), 0)
    limit = jnp.zeros(row.shape, jnp.int32)
    for b in range(keys.shape[0] // BLOCK):
        limit = jnp.where(row >= b * BLOCK, live[line * 8 + 2 * b + core] + b * BLOCK, limit)
    return jnp.where(row < limit, jnp.exp(scores * (1.0 / math.sqrt(HEAD))), 0.0)


def from_core(core):
    return pl.BlockSpec((1, 4, 1, BLOCK, HEAD), lambda i, live: (i, 0, core, 0, 0))


def fill(queries, slots):
    n = slots[0].shape[0]
    for j, slot in enumerate(slots):
        queries[j * n : (j + 1) * n, :] = slot[...]


def score_kernel(live, q0, q1, q2, q3, keys, weight, den, queries):
    step = pl.program_id(0)

    @pl.when(step == 0)
    def _():
        fill(queries, (q0, q1, q2, q3))
        den[...] = jnp.zeros_like(den)

    e = exp_scores(live, step, 0, keys[...].reshape(-1, HEAD), queries[...])
    den[...] += jnp.sum(e, axis=0, keepdims=True)
    weight[...] = e.astype(BF16)


def score(live, slots, arrived):
    n = 4 * slots[0].shape[0]
    keys = 4 * BLOCK
    return pl.pallas_call(
        score_kernel,
        grid_spec=pltpu.PrefetchScalarGridSpec(
            num_scalar_prefetch=1,
            grid=(4,),
            in_specs=[pl.BlockSpec((n // 4, HEAD), lambda i, live: (0, 0))] * 4 + [from_core(0)],
            out_specs=(
                pl.BlockSpec((keys, n), lambda i, live: (i, 0)),
                pl.BlockSpec((1, n), lambda i, live: (0, 0)),
            ),
            scratch_shapes=[pltpu.VMEM((n, HEAD), BF16)],
        ),
        out_shape=(jax.ShapeDtypeStruct((4 * keys, n), BF16), jax.ShapeDtypeStruct((1, n), F32)),
        compiler_params=params(),
        cost_estimate=pl.CostEstimate(
            flops=8 * keys * n * HEAD, bytes_accessed=4 * keys * n * 2, transcendentals=4 * keys * n
        ),
        name="score",
    )(live, *slots, arrived)


EXTRA = 16


def mix_kernel(live, q0, q1, q2, q3, keys, values, weight, weight_values, den, o0, o1, o2, o3, queries, acc, bottom):
    step = pl.program_id(0)

    @pl.when(step == 0)
    def _():
        fill(queries, (q0, q1, q2, q3))

    e = exp_scores(live, step, 1, keys[...].reshape(-1, HEAD), queries[...])
    here = jnp.sum(e, axis=0, keepdims=True)
    part = 0.0
    for v, w in ((weight_values, weight[...]), (values, e.astype(BF16))):
        flipped = v[...].reshape(-1, HEAD).astype(F32).T.astype(BF16)
        part += lax.dot_general(flipped, w, (((1,), (0,)), ((), ())), preferred_element_type=F32)

    @pl.when(step == 0)
    def _():
        acc[...] = part
        bottom[...] = den[...] + here

    @pl.when(step > 0)
    def _():
        acc[...] += part
        bottom[...] += here

    @pl.when(step == pl.num_programs(0) - 1)
    def _():
        n = o0.shape[1]
        row = lax.broadcasted_iota(jnp.int32, (EXTRA, n), 0)
        for j, out in enumerate((o0, o1, o2, o3)):
            at = slice(j * n, (j + 1) * n)
            out[:HEAD, :] = acc[:, at].astype(BF16)
            d = bottom[:, at]
            coarse = d.astype(BF16).astype(F32)
            tail = jnp.where(row == 0, coarse, jnp.where(row == 1, d - coarse, 0.0))
            out[HEAD:, :] = tail.astype(BF16)


def mix(live, slots, first, second, weight, den):
    total, n = weight.shape
    keys = total // 4
    out = jax.ShapeDtypeStruct((HEAD + EXTRA, n // 4), BF16)
    return pl.pallas_call(
        mix_kernel,
        grid_spec=pltpu.PrefetchScalarGridSpec(
            num_scalar_prefetch=1,
            grid=(4,),
            in_specs=[pl.BlockSpec((n // 4, HEAD), lambda i, live: (0, 0))] * 4
            + [
                from_core(1),
                from_core(1),
                pl.BlockSpec((keys, n), lambda i, live: (i, 0)),
                from_core(0),
                pl.BlockSpec((1, n), lambda i, live: (0, 0)),
            ],
            out_specs=(pl.BlockSpec(out.shape, lambda i, live: (0, 0)),) * 4,
            scratch_shapes=[pltpu.VMEM((n, HEAD), BF16), pltpu.VMEM((HEAD, n), F32), pltpu.VMEM((1, n), F32)],
        ),
        out_shape=(out,) * 4,
        compiler_params=params(),
        cost_estimate=pl.CostEstimate(
            flops=6 * total * n * HEAD, bytes_accessed=total * n * 2, transcendentals=total * n
        ),
        name="mix",
    )(live, *slots, second, first, weight, second, den)


def join_kernel(m0, m1, m2, m3, num, den, out):
    acc = num[...]
    bottom = den[...]
    for m in (m0, m1, m2, m3):
        acc = acc + m[:HEAD, :].astype(F32)
        bottom = bottom + jnp.sum(m[HEAD:, :].astype(F32), axis=0, keepdims=True)
    result = (acc / bottom).T.astype(BF16)
    rows = out.shape[0]
    for head in range(out.shape[1] // HEAD):
        out[:, head * HEAD : (head + 1) * HEAD] = result[head * rows : (head + 1) * rows, :]


def join(messages, num, den, rows):
    n = num.shape[1]
    return pl.pallas_call(
        join_kernel,
        out_shape=jax.ShapeDtypeStruct((rows, n // rows * HEAD), BF16),
        compiler_params=params(),
        name="join",
    )(*messages, num, den)


def on_device(hidden, lengths, owner, w_key, w_value, k_gain, q_gain, dq, dk, dv):
    zh, y, c = lax.axis_index("zh"), lax.axis_index("y"), lax.axis_index("c")
    zl, t = lax.axis_index("zl"), lax.axis_index("x")
    _, prompts, block, width = hidden.shape
    hidden = hidden.reshape(4, prompts // 4 * block, width)
    blocks = 4 * prompts

    w_first = jnp.where(c == 0, w_key, w_value)
    line = [lax.ppermute(w_first, Z_CORE, shift_core(*steps)) for steps in ((1, 1), (-1, -1), (2, -2))]
    w_key, w_value, *line = lax.optimization_barrier((w_key, w_value, *line))
    w_second = jnp.where(c == 0, w_value, w_key)
    core = [lax.ppermute(piece, "c", ((0, 1), (1, 0))) for piece in line]

    delta = jnp.array(DELTA, jnp.int32)
    order = (zh + delta) % 4

    sent = ((t ^ 1, 3 - (t ^ 1)), (3 - t, (3 - t) ^ 1))
    kept = ((t, 3 - t), (t, t ^ 1))

    def info(*pairs):
        heads = jnp.stack([head for pair in pairs for head in pair])
        ahead = (heads - zl) % 4
        place = jnp.where(ahead == 0, 0, jnp.where(ahead == 3, 1, ahead + 1))
        return jnp.concatenate([order, place]).astype(jnp.int32)

    yc = jnp.arange(8, dtype=jnp.int32)
    prompt_of = (order[:, None] * 8 + yc[None, :]).reshape(-1)
    my_block = ((zh * 8 + y * 2 + c) * 4 + zl).astype(jnp.int32)
    block_at = (my_block - owner[prompt_of]) % blocks
    my_length = lengths[zh * 8 + y * 2 + c]
    step = jnp.arange(dk.shape[1] * dk.shape[2], dtype=jnp.int32) % dk.shape[2]
    positions = jnp.concatenate([block_at * block, jnp.arange(block, dtype=jnp.int32), my_length + step])
    lane = jnp.arange(HEAD, dtype=jnp.int32)
    frequency = jnp.exp((lane % (HEAD // 2)).astype(F32) * (-2.0 * math.log(1000000.0) / HEAD))
    angles = positions.astype(F32)[:, None] * frequency
    cos = jnp.cos(angles)
    sin = jnp.sin(angles) * jnp.where(lane < HEAD // 2, -1.0, 1.0)
    cut = (prompts, prompts + block)

    rows = dk.shape[1] * dk.shape[2]
    q_mine, num_new, den_new = prep(
        dq.reshape(rows, -1),
        dk.reshape(rows, HEAD),
        dv.reshape(rows, HEAD),
        q_gain[None],
        k_gain[None],
        cos[cut[1] :],
        sin[cut[1] :],
    )

    pieces = (w_first, *line)
    send_a, send_b = project((2, 2), info(*sent), hidden, pieces)
    keep_a, keep_b = project((2, 2), info(*kept), hidden, pieces)
    both = info(sent[0], kept[0], sent[1], kept[1])
    next_a, after_a, next_b, after_b = project((3, 2, 3, 2), both, hidden, (w_second, *core))

    in_a = lax.ppermute(send_a, "x", PAIRS[0])
    in_b = lax.ppermute(send_b, "x", PAIRS[1])
    routes = home_routes()
    q_mine, in_a, in_b = lax.optimization_barrier((q_mine, in_a, in_b))
    queries = [lax.ppermute(q_mine, Z_LINE, [(b, a) for a, b in route]) for route in routes]
    sum_a = lax.ppermute(pair_sum(keep_a, in_a, next_b), "x", PAIRS[1])
    sum_b = lax.ppermute(pair_sum(keep_b, in_b, next_a), "x", PAIRS[0])
    sum_a, sum_b, *queries = lax.optimization_barrier((sum_a, sum_b, *queries))
    tail_a = lax.ppermute(pair_sum(after_a, sum_b), "x", PAIRS[1])
    tail_b = lax.ppermute(pair_sum(after_b, sum_a), "x", PAIRS[0])
    tables = (k_gain[None], cos[: cut[0]], sin[: cut[0]], cos[cut[0] : cut[1]], sin[cut[0] : cut[1]])
    second_type = jnp.reshape(c, (1,)).astype(jnp.int32)
    page_first = finish(1 - second_type, (keep_a, in_a, sum_a, keep_b, in_b, sum_b), (0, 0, 0), tables)
    page_second = finish(second_type, (after_a, sum_b, tail_a, after_b, sum_a, tail_b), (0, 1, 0), tables)

    def spread(page):
        page = page.reshape(prompts, block, HEAD)
        got = lax.all_to_all(page, Z_GROUP, split_axis=0, concat_axis=0, tiled=True)
        return got.reshape(4, 4, 2, block, HEAD)

    first = spread(page_first)
    second = spread(page_second)

    prompt = order[zl] * 8 + y * 2 + c
    sources = (zh * 8 + yc[None, :]) * 4 + jnp.arange(4, dtype=jnp.int32)[:, None]
    source_at = (sources.reshape(-1) - owner[prompt]) % blocks
    live = jnp.clip(lengths[prompt] - source_at * block, 0, block)
    live = live.astype(jnp.int32)
    weight, den = score(live, queries, first)
    messages = mix(live, queries, first, second, weight, den)
    back = [lax.ppermute(m, Z_LINE, route) for m, route in zip(messages, routes)]
    out = join(back, num_new, den_new, rows)
    return out.reshape(dq.shape)


def solution(mesh):
    fine = Mesh(mesh.devices.reshape(4, 4, 2, 4, 4), ("zh", "y", "c", "zl", "x"))
    fork = ("zh", "y", "c")
    rows = P(fork, "zl", None, "x")
    in_specs = (
        P(fork, None, "zl", "x"),
        P(),
        P(),
        P("x", "zl"),
        P("x", "zl"),
        P(),
        P(),
        rows,
        rows,
        rows,
    )
    return jax.shard_map(on_device, mesh=fine, in_specs=in_specs, out_specs=rows, check_vma=False)
```

```python
import functools
import math

import jax
import jax.numpy as jnp
from jax import lax
from jax.experimental import pallas as pl
from jax.experimental.pallas import tpu as pltpu
from jax.sharding import Mesh, PartitionSpec as P

BF16 = jnp.bfloat16
F32 = jnp.float32
HEAD = 128
BLOCK = 64
COST = (10**7, 15 * 10**9, 3 * 10**9, 20 * 10**9)
DELTA = (3, 0, 2, 1)
Z_GROUP = ("zl", "y", "c")
Z_LINE = ("zh", "zl")
Z_CORE = ("zh", "c", "zl")
PAIRS = (
    ((0, 1), (1, 0), (2, 3), (3, 2)),
    ((0, 3), (3, 0), (1, 2), (2, 1)),
)


def shift_core(step0, step1):
    place = lambda z, c: (z % 16 // 4 * 2 + c) * 4 + z % 4
    return [(place(z, c), place(z + step, c)) for z in range(16) for c, step in enumerate((step0, step1))]


def home_routes():
    routes = [[] for _ in range(4)]
    for group in range(4):
        for place, delta in enumerate(DELTA):
            prompt_group = (group + delta) % 4
            for rep in range(4):
                routes[(rep + delta) % 4].append((group * 4 + place, prompt_group * 4 + rep))
    return routes


def swap_groups():
    return [(h * 4 + l, (h + d) % 4 * 4 + l ^ m) for h in range(4) for l, (d, m) in enumerate(((3, 3), (0, 0), (2, 0), (1, 3)))]


def params(mib=20):
    return pltpu.CompilerParams(vmem_limit_bytes=mib * 2**20)


def rms_scale(v):
    return v * lax.rsqrt(jnp.mean(v * v, axis=-1, keepdims=True) + 1e-06)


def turn(v, cos, sin):
    return v * cos + pltpu.roll(v, HEAD // 2, 1) * sin


def prep_kernel(dq, dk, dv, qg, kg, cos, sin, q_out, num_out, den_out):
    heads = dq.shape[1] // HEAD
    rows = dq.shape[0]
    cos, sin = cos[...], sin[...]
    for head in range(heads):
        v = dq[:, head * HEAD : (head + 1) * HEAD].astype(F32)
        q_out[head * rows : (head + 1) * rows, :] = turn(rms_scale(v) * qg[...], cos, sin).astype(BF16)
    key = turn(rms_scale(dk[...].astype(F32)) * kg[...], cos, sin).astype(BF16)
    scores = lax.dot_general(key, q_out[...], (((1,), (1,)), ((), ())), preferred_element_type=F32)
    k_row = lax.broadcasted_iota(jnp.int32, scores.shape, 0)
    q_col = lax.broadcasted_iota(jnp.int32, scores.shape, 1) & (rows - 1)
    seen = ((k_row >> 3) == (q_col >> 3)) & ((k_row & 7) <= (q_col & 7))
    weight = jnp.where(seen, jnp.exp(scores * (1.0 / math.sqrt(HEAD))), 0.0)
    den_out[...] = jnp.sum(weight, axis=0, keepdims=True)
    num_out[...] = lax.dot_general(
        dv[...].astype(F32).T.astype(BF16), weight.astype(BF16), (((1,), (0,)), ((), ())), preferred_element_type=F32
    )


def prep(dq, dk, dv, qg, kg, cos, sin):
    rows = dq.shape[0]
    n = dq.shape[1] // HEAD * rows
    return pl.pallas_call(
        prep_kernel,
        out_shape=(
            jax.ShapeDtypeStruct((n, HEAD), BF16),
            jax.ShapeDtypeStruct((HEAD, n), F32),
            jax.ShapeDtypeStruct((1, n), F32),
        ),
        compiler_params=params(),
        name="prep",
    )(dq, dk, dv, qg, kg, cos, sin)


def project_half(info, i, x, group, w, out):
    both = jnp.concatenate([w[info[2 * i]], w[info[2 * i + 1]]], axis=1)
    n = x.shape[1]
    for k in range(2):
        y = jnp.dot(x[group + k], both, preferred_element_type=F32).astype(BF16)
        out[0, k * n : (k + 1) * n, :] = y[:, :HEAD]
        out[1, k * n : (k + 1) * n, :] = y[:, HEAD:]


def load_kernel(info, hidden, p0, p1, p2, p3, out_a, out_b, x, w, wsem, xsem):
    weights = [pltpu.make_async_copy(p, w.at[j], wsem.at[j]) for j, p in enumerate((p0, p1, p2, p3))]
    states = [pltpu.make_async_copy(hidden.at[info[4 + i]], x.at[i], xsem.at[i]) for i in range(4)]
    for copy in weights + states:
        copy.start()
    for copy in weights:
        copy.wait()
    for half, out in enumerate((out_a, out_b)):
        for copy in states[2 * half : 2 * half + 2]:
            copy.wait()
        project_half(info, half, x, 2 * half, w, out)


def more_kernel(info, x, w, out_a, out_b):
    for half, out in enumerate((out_a, out_b)):
        project_half(info, half, x, 2 * half, w, out)


def next_kernel(info, x, p0, p1, p2, p3, out_a, more_a, out_b, more_b, w, wsem):
    weights = [pltpu.make_async_copy(p, w.at[j], wsem.at[j]) for j, p in enumerate((p0, p1, p2, p3))]
    for copy in weights:
        copy.start()
    for copy in weights:
        copy.wait()
    for i, out in enumerate((out_a, more_a, out_b, more_b)):
        project_half(info, i, x, i // 2 * 2, w, out)


SMEM, VMEM, ANY = (pl.BlockSpec(memory_space=m) for m in (pltpu.SMEM, pltpu.VMEM, pl.ANY))


def project(kernel, outs, in_specs, scratch, name, *args):
    return pl.pallas_call(
        kernel,
        in_specs=in_specs,
        out_specs=[VMEM] * len(outs),
        out_shape=[jax.ShapeDtypeStruct(shape, BF16) for shape in outs],
        scratch_shapes=scratch,
        compiler_params=params(24),
        cost_estimate=pl.CostEstimate(flops=COST[2], bytes_accessed=2**20, transcendentals=0),
        name=name,
    )(*args)


def pair_sum_kernel(keep, first, out):
    out[...] = (keep[0].astype(F32) + first[0].astype(F32)).astype(BF16)


def pair_sum(keep, first):
    rows = keep.shape[1]
    other = pl.BlockSpec((1, rows, HEAD), lambda i: (1, 0, 0))
    return pl.pallas_call(
        pair_sum_kernel,
        grid=(1,),
        in_specs=[other, other],
        out_specs=pl.BlockSpec((rows, HEAD), lambda i: (0, 0)),
        out_shape=jax.ShapeDtypeStruct((rows, HEAD), BF16),
        compiler_params=params(),
        name="pair_sum",
    )(keep, first)


def finish_kernel(is_key, ka, ra, sa, kb, rb, sb, gain, cos_b, sin_b, cos_i, sin_i, out):
    step = pl.program_id(0)

    def run(keep, first, second):
        total = keep[0].astype(F32) + first[0].astype(F32) + second[...].astype(F32)

        @pl.when(is_key[0] == 0)
        def _():
            out[...] = total.astype(BF16)

        @pl.when(is_key[0] == 1)
        def _():
            scaled = rms_scale(total) * gain[...]
            ci, si = cos_i[...], sin_i[...]
            for b in range(total.shape[0] // BLOCK):
                cb, sb_ = cos_b[b : b + 1, :], sin_b[b : b + 1, :]
                cos = cb * ci - sb_ * si
                sin = sb_ * ci + cb * si
                out[b * BLOCK : (b + 1) * BLOCK, :] = turn(scaled[b * BLOCK : (b + 1) * BLOCK, :], cos, sin).astype(BF16)

    @pl.when(step < 2)
    def _():
        run(ka, ra, sa)

    @pl.when(step >= 2)
    def _():
        run(kb, rb, sb)


def finish(is_key, parts, extra, cost):
    rows = parts[0].shape[1] // 2
    low = lambda i: jnp.minimum(i, 1)
    high = lambda i: jnp.maximum(i - 2, 0)
    specs = []
    for place in (low, high):
        own = pl.BlockSpec((1, rows, HEAD), lambda i, k, place=place: (0, place(i), 0))
        specs += [own, own, pl.BlockSpec((rows, HEAD), lambda i, k, place=place: (place(i), 0))]
    per = pl.BlockSpec((rows // BLOCK, HEAD), lambda i, k: (i, 0))
    whole = lambda a: pl.BlockSpec(a.shape, lambda i, k: (0, 0))
    specs += [whole(extra[0]), per, per, whole(extra[3]), whole(extra[4])]
    return pl.pallas_call(
        finish_kernel,
        grid_spec=pltpu.PrefetchScalarGridSpec(
            num_scalar_prefetch=1,
            grid=(4,),
            in_specs=specs,
            out_specs=pl.BlockSpec((rows, HEAD), lambda i, k: (i, 0)),
        ),
        out_shape=jax.ShapeDtypeStruct((4 * rows, HEAD), BF16),
        compiler_params=params(),
        cost_estimate=pl.CostEstimate(flops=cost, bytes_accessed=2**20, transcendentals=0),
        name="finish",
    )(is_key, *parts, *extra)


def exp_scores(live, line, core, keys, queries):
    scores = lax.dot_general(keys, queries, (((1,), (1,)), ((), ())), preferred_element_type=F32)
    row = lax.broadcasted_iota(jnp.int32, (keys.shape[0], 1), 0)
    limit = jnp.zeros(row.shape, jnp.int32)
    for b in range(keys.shape[0] // BLOCK):
        limit = jnp.where(row >= b * BLOCK, live[line * 8 + 2 * b + core] + b * BLOCK, limit)
    return jnp.where(row < limit, jnp.exp(scores * (1.0 / math.sqrt(HEAD))), 0.0)


def from_core(core):
    return pl.BlockSpec((1, 4, 1, BLOCK, HEAD), lambda i, live: (i, 0, core, 0, 0))


def score_kernel(live, queries, keys, weight, den):
    step = pl.program_id(0)

    @pl.when(step == 0)
    def _():
        den[...] = jnp.zeros_like(den)

    e = exp_scores(live, step, 0, keys[...].reshape(-1, HEAD), queries[...])
    den[...] += jnp.sum(e, axis=0, keepdims=True)
    weight[...] = e.astype(BF16)


def score(live, queries, arrived):
    n = queries.shape[0]
    keys = 4 * BLOCK
    return pl.pallas_call(
        score_kernel,
        grid_spec=pltpu.PrefetchScalarGridSpec(
            num_scalar_prefetch=1,
            grid=(4,),
            in_specs=[pl.BlockSpec((n, HEAD), lambda i, live: (0, 0)), from_core(0)],
            out_specs=(
                pl.BlockSpec((keys, n), lambda i, live: (i, 0)),
                pl.BlockSpec((1, n), lambda i, live: (0, 0)),
            ),
        ),
        out_shape=(jax.ShapeDtypeStruct((4 * keys, n), BF16), jax.ShapeDtypeStruct((1, n), F32)),
        compiler_params=params(),
        cost_estimate=pl.CostEstimate(
            flops=COST[3], bytes_accessed=2**20, transcendentals=0
        ),
        name="score",
    )(live, queries, arrived)


EXTRA = 16


def mix_kernel(live, queries, keys, values, weight, weight_values, den, o0, o1, o2, o3, acc, bottom):
    step = pl.program_id(0)

    e = exp_scores(live, step, 1, keys[...].reshape(-1, HEAD), queries[...])
    here = jnp.sum(e, axis=0, keepdims=True)
    part = 0.0
    for v, w in ((weight_values, weight[...]), (values, e.astype(BF16))):
        flipped = v[...].reshape(-1, HEAD).astype(F32).T.astype(BF16)
        part += lax.dot_general(flipped, w, (((1,), (0,)), ((), ())), preferred_element_type=F32)

    @pl.when(step == 0)
    def _():
        acc[...] = part
        bottom[...] = den[...] + here

    @pl.when(step > 0)
    def _():
        acc[...] += part
        bottom[...] += here

    @pl.when(step == pl.num_programs(0) - 1)
    def _():
        n = o0.shape[1]
        row = lax.broadcasted_iota(jnp.int32, (EXTRA, n), 0)
        for j, out in enumerate((o0, o1, o2, o3)):
            at = pl.ds(pl.multiple_of(((live[32] + j) & 3) * n, n), n)
            out[:HEAD, :] = acc[:, at].astype(BF16)
            d = bottom[:, at]
            coarse = d.astype(BF16).astype(F32)
            tail = jnp.where(row == 0, coarse, jnp.where(row == 1, d - coarse, 0.0))
            out[HEAD:, :] = tail.astype(BF16)


def mix(live, queries, first, second, weight, den):
    total, n = weight.shape
    keys = total // 4
    out = jax.ShapeDtypeStruct((HEAD + EXTRA, n // 4), BF16)
    return pl.pallas_call(
        mix_kernel,
        grid_spec=pltpu.PrefetchScalarGridSpec(
            num_scalar_prefetch=1,
            grid=(4,),
            in_specs=[
                pl.BlockSpec((n, HEAD), lambda i, live: (0, 0)),
                from_core(1),
                from_core(1),
                pl.BlockSpec((keys, n), lambda i, live: (i, 0)),
                from_core(0),
                pl.BlockSpec((1, n), lambda i, live: (0, 0)),
            ],
            out_specs=(pl.BlockSpec(out.shape, lambda i, live: (0, 0)),) * 4,
            scratch_shapes=[pltpu.VMEM((HEAD, n), F32), pltpu.VMEM((1, n), F32)],
        ),
        out_shape=(out,) * 4,
        compiler_params=params(),
        cost_estimate=pl.CostEstimate(
            flops=6 * total * n * HEAD, bytes_accessed=total * n * 2, transcendentals=total * n
        ),
        name="mix",
    )(live, queries, second, first, weight, second, den)


def join_kernel(m0, m1, m2, m3, num, den, out):
    acc = num[...]
    bottom = den[...]
    for m in (m0, m1, m2, m3):
        acc = acc + m[:HEAD, :].astype(F32)
        bottom = bottom + jnp.sum(m[HEAD:, :].astype(F32), axis=0, keepdims=True)
    result = (acc / bottom).T.astype(BF16)
    rows = out.shape[0]
    for head in range(out.shape[1] // HEAD):
        out[:, head * HEAD : (head + 1) * HEAD] = result[head * rows : (head + 1) * rows, :]


def join(messages, num, den, rows):
    n = num.shape[1]
    return pl.pallas_call(
        join_kernel,
        out_shape=jax.ShapeDtypeStruct((rows, n // rows * HEAD), BF16),
        compiler_params=params(),
        name="join",
    )(*messages, num, den)


def on_device(hidden, lengths, owner, w_key, w_value, k_gain, q_gain, dq, dk, dv):
    zh, y, c = lax.axis_index("zh"), lax.axis_index("y"), lax.axis_index("c")
    zl, t = lax.axis_index("zl"), lax.axis_index("x")
    _, prompts, block, width = hidden.shape
    hidden = hidden.reshape(4, prompts // 4 * block, width)
    blocks = 4 * prompts

    w_first = jnp.where(c == 0, w_key, w_value)
    line = [lax.ppermute(w_first, Z_CORE, shift_core(*steps)) for steps in ((1, 1), (-1, -1), (2, -2))]
    delta = jnp.array(DELTA, jnp.int32)
    order = (zh + delta) % 4

    sent = ((t ^ 1, 3 - (t ^ 1)), (3 - t, (3 - t) ^ 1))
    kept = ((t, 3 - t), (t, t ^ 1))

    def info(*pairs):
        heads = jnp.stack([head for pair in pairs for head in pair])
        ahead = (heads - zl) % 4
        place = jnp.where(ahead == 0, 0, jnp.where(ahead == 3, 1, ahead + 1))
        return place.astype(jnp.int32)

    yc = jnp.arange(8, dtype=jnp.int32)
    my_block = ((zh * 8 + y * 2 + c) * 4 + zl).astype(jnp.int32)
    of_group = jnp.arange(4, dtype=jnp.int32)[None, :, None] == order[:, None, None]
    owners = jnp.sum(jnp.where(of_group, owner.reshape(4, 8)[None], 0), axis=1).reshape(-1)
    block_at = (my_block - owners) % blocks
    pick = lambda table, at: jnp.sum(jnp.where(jnp.arange(prompts, dtype=jnp.int32) == at, table, 0))
    my_length = pick(lengths, zh * 8 + y * 2 + c)
    step = jnp.arange(dk.shape[1] * dk.shape[2], dtype=jnp.int32) % dk.shape[2]
    positions = jnp.concatenate([block_at * block, jnp.arange(block, dtype=jnp.int32), my_length + step])
    lane = jnp.arange(HEAD, dtype=jnp.int32)
    frequency = jnp.exp((lane % (HEAD // 2)).astype(F32) * (-2.0 * math.log(1000000.0) / HEAD))
    angles = positions.astype(F32)[:, None] * frequency
    cos = jnp.cos(angles)
    sin = jnp.sin(angles) * jnp.where(lane < HEAD // 2, -1.0, 1.0)
    cut = (prompts, prompts + block)

    rows = dk.shape[1] * dk.shape[2]
    q_mine, num_new, den_new = prep(
        dq.reshape(rows, -1),
        dk.reshape(rows, HEAD),
        dv.reshape(rows, HEAD),
        q_gain[None],
        k_gain[None],
        cos[cut[1] :],
        sin[cut[1] :],
    )

    def join_with(piece, bit):
        other = lax.ppermute(piece, "zl", [(i, i ^ bit) for i in range(4)])
        low = (zl & bit) == 0
        return jnp.concatenate([jnp.where(low, piece, other), jnp.where(low, other, piece)])

    queries = join_with(q_mine, 1)
    queries, cos, sin, *line = lax.optimization_barrier((queries, cos, sin, *line))

    width = w_key.shape[0]
    half_rows = 2 * hidden.shape[1]
    part = (2, half_rows, HEAD)
    tall = (4, width, HEAD)
    four = pltpu.SemaphoreType.DMA((4,))
    send_a, send_b, states, weights = project(
        load_kernel,
        (part, part, hidden.shape, tall),
        [SMEM, pl.BlockSpec(memory_space=pltpu.HBM)] + [ANY] * 4,
        [four, four],
        "project_load",
        jnp.concatenate([info(*sent), order]).astype(jnp.int32),
        hidden,
        w_first,
        *line,
    )
    queries, send_a, send_b = lax.optimization_barrier((queries, send_a, send_b))
    queries = join_with(queries, 2)
    keep_a, keep_b = project(
        more_kernel, (part, part), [SMEM, VMEM, VMEM], [], "project_more", info(*kept), states, weights
    )
    w_key, w_value, send_a, send_b, *line = lax.optimization_barrier((w_key, w_value, send_a, send_b, *line))
    w_second = jnp.where(c == 0, w_value, w_key)
    core = lax.ppermute(jnp.concatenate(line), "c", ((0, 1), (1, 0)))
    next_a, after_a, next_b, after_b = project(
        next_kernel,
        (part,) * 4,
        [SMEM, VMEM] + [ANY] * 4,
        [pltpu.VMEM(tall, BF16), four],
        "project_next",
        info(sent[0], kept[0], sent[1], kept[1]),
        states,
        w_second,
        *(core[i * width : (i + 1) * width] for i in range(3)),
    )
    keep_a, keep_b, next_a, next_b = lax.optimization_barrier((keep_a, keep_b, next_a, next_b))

    in_a = lax.ppermute(send_a, "x", PAIRS[0])
    in_b = lax.ppermute(send_b, "x", PAIRS[1])
    sum_a, sum_b = pair_sum(keep_a, in_a), pair_sum(keep_b, in_b)
    sum_a, sum_b, next_a, next_b, queries = lax.optimization_barrier((sum_a, sum_b, next_a, next_b, queries))
    last_a = lax.ppermute(sum_a, "x", PAIRS[1])
    last_b = lax.ppermute(sum_b, "x", PAIRS[0])
    then_a = lax.ppermute(next_a, "x", PAIRS[0])
    then_b = lax.ppermute(next_b, "x", PAIRS[1])
    then_a, then_b, queries = lax.optimization_barrier((then_a, then_b, queries))
    queries = lax.ppermute(queries, Z_LINE, swap_groups())
    tail_a = lax.ppermute(pair_sum(after_a, then_a), "x", PAIRS[1])
    tail_b = lax.ppermute(pair_sum(after_b, then_b), "x", PAIRS[0])
    tables = (k_gain[None], cos[: cut[0]], sin[: cut[0]], cos[cut[0] : cut[1]], sin[cut[0] : cut[1]])
    second_type = jnp.reshape(c, (1,)).astype(jnp.int32)
    page_first = finish(1 - second_type, (keep_a, in_a, last_a, keep_b, in_b, last_b), tables, COST[0])
    page_second = finish(second_type, (after_a, then_a, tail_a, after_b, then_b, tail_b), tables, COST[1])

    def spread(page):
        page = page.reshape(prompts, block, HEAD)
        got = lax.all_to_all(page, Z_GROUP, split_axis=0, concat_axis=0, tiled=True)
        return got.reshape(4, 4, 2, block, HEAD)

    first = spread(page_first)
    second = spread(page_second)

    group = (zh + jnp.where(zl == 0, 3, jnp.where(zl == 1, 0, jnp.where(zl == 2, 2, 1)))) % 4
    prompt = group * 8 + y * 2 + c
    sources = (zh * 8 + yc[None, :]) * 4 + jnp.arange(4, dtype=jnp.int32)[:, None]
    source_at = (sources.reshape(-1) - pick(owner, prompt)) % blocks
    live = jnp.clip(pick(lengths, prompt) - source_at * block, 0, block)
    live = jnp.concatenate([live, ((zh - group) % 4)[None]]).astype(jnp.int32)
    weight, den = score(live, queries, first)
    messages = mix(live, queries, first, second, weight, den)
    back = [lax.ppermute(m, Z_LINE, route) for m, route in zip(messages, home_routes())]
    out = join(back, num_new, den_new, rows)
    return out.reshape(dq.shape)


def solution(mesh):
    fine = Mesh(mesh.devices.reshape(4, 4, 2, 4, 4), ("zh", "y", "c", "zl", "x"))
    fork = ("zh", "y", "c")
    rows = P(fork, "zl", None, "x")
    in_specs = (
        P(fork, None, "zl", "x"),
        P(),
        P(),
        P("x", "zl"),
        P("x", "zl"),
        P(),
        P(),
        rows,
        rows,
        rows,
    )
    return jax.shard_map(on_device, mesh=fine, in_specs=in_specs, out_specs=rows, check_vma=False)
```

```python
import functools
import math

import jax
import jax.numpy as jnp
from jax import lax
from jax.experimental import pallas as pl
from jax.experimental.pallas import tpu as pltpu
from jax.sharding import Mesh, PartitionSpec as P

BF16 = jnp.bfloat16
F32 = jnp.float32
HEAD = 128
BLOCK = 64
COST = (10**7, 15 * 10**9, 3 * 10**9, 20 * 10**9)
DELTA = (3, 0, 2, 1)
Z_GROUP = ("zl", "y", "c")
Z_LINE = ("zh", "zl")
Z_CORE = ("zh", "c", "zl")
PAIRS = (
    ((0, 1), (1, 0), (2, 3), (3, 2)),
    ((0, 3), (3, 0), (1, 2), (2, 1)),
)


def shift_core(step0, step1):
    place = lambda z, c: (z % 16 // 4 * 2 + c) * 4 + z % 4
    return [(place(z, c), place(z + step, c)) for z in range(16) for c, step in enumerate((step0, step1))]


def home_routes():
    routes = [[] for _ in range(4)]
    for group in range(4):
        for place, delta in enumerate(DELTA):
            prompt_group = (group + delta) % 4
            for rep in range(4):
                routes[(rep + delta) % 4].append((group * 4 + place, prompt_group * 4 + rep))
    return routes


def swap_groups():
    return [(h * 4 + l, (h + d) % 4 * 4 + l ^ m) for h in range(4) for l, (d, m) in enumerate(((3, 3), (0, 0), (2, 0), (1, 3)))]


def params(mib=8):
    return pltpu.CompilerParams(vmem_limit_bytes=mib * 2**20)


def rms_scale(v):
    return v * lax.rsqrt(jnp.mean(v * v, axis=-1, keepdims=True) + 1e-06)


def turn(v, cos, sin):
    return v * cos + pltpu.roll(v, HEAD // 2, 1) * sin


def prep_kernel(dq, dk, dv, qg, kg, cos, sin, q_out, num_out, den_out):
    heads = dq.shape[1] // HEAD
    rows = dq.shape[0]
    cos, sin = cos[...], sin[...]
    for head in range(heads):
        v = dq[:, head * HEAD : (head + 1) * HEAD].astype(F32)
        q_out[head * rows : (head + 1) * rows, :] = turn(rms_scale(v) * qg[...], cos, sin).astype(BF16)
    key = turn(rms_scale(dk[...].astype(F32)) * kg[...], cos, sin).astype(BF16)
    scores = lax.dot_general(key, q_out[...], (((1,), (1,)), ((), ())), preferred_element_type=F32)
    k_row = lax.broadcasted_iota(jnp.int32, scores.shape, 0)
    q_col = lax.broadcasted_iota(jnp.int32, scores.shape, 1) & (rows - 1)
    seen = ((k_row >> 3) == (q_col >> 3)) & ((k_row & 7) <= (q_col & 7))
    weight = jnp.where(seen, jnp.exp(scores * (1.0 / math.sqrt(HEAD))), 0.0)
    den_out[...] = jnp.sum(weight, axis=0, keepdims=True)
    num_out[...] = lax.dot_general(
        dv[...].astype(F32).T.astype(BF16), weight.astype(BF16), (((1,), (0,)), ((), ())), preferred_element_type=F32
    )


def prep(dq, dk, dv, qg, kg, cos, sin):
    rows = dq.shape[0]
    n = dq.shape[1] // HEAD * rows
    return pl.pallas_call(
        prep_kernel,
        out_shape=(
            jax.ShapeDtypeStruct((n, HEAD), BF16),
            jax.ShapeDtypeStruct((HEAD, n), F32),
            jax.ShapeDtypeStruct((1, n), F32),
        ),
        compiler_params=params(59),
        name="prep",
    )(dq, dk, dv, qg, kg, cos, sin)


def project_half(info, i, x, group, w, out):
    both = jnp.concatenate([w[info[2 * i]], w[info[2 * i + 1]]], axis=1)
    n = x.shape[1]
    for k in range(2):
        y = jnp.dot(x[group + k], both, preferred_element_type=F32).astype(BF16)
        out[0, k * n : (k + 1) * n, :] = y[:, :HEAD]
        out[1, k * n : (k + 1) * n, :] = y[:, HEAD:]


def load_kernel(info, hidden, p0, p1, p2, p3, out_a, out_b, x, w, wsem, xsem):
    weights = [pltpu.make_async_copy(p, w.at[j], wsem.at[j]) for j, p in enumerate((p0, p1, p2, p3))]
    states = [pltpu.make_async_copy(hidden.at[info[4 + i]], x.at[i], xsem.at[i]) for i in range(4)]
    for copy in weights + states:
        copy.start()
    for copy in weights:
        copy.wait()
    for half, out in enumerate((out_a, out_b)):
        for copy in states[2 * half : 2 * half + 2]:
            copy.wait()
        project_half(info, half, x, 2 * half, w, out)


def more_kernel(info, x, w, out_a, out_b):
    for half, out in enumerate((out_a, out_b)):
        project_half(info, half, x, 2 * half, w, out)


def next_kernel(info, x, p0, p1, p2, p3, out_a, more_a, out_b, more_b, w, wsem):
    weights = [pltpu.make_async_copy(p, w.at[j], wsem.at[j]) for j, p in enumerate((p0, p1, p2, p3))]
    for copy in weights:
        copy.start()
    for copy in weights:
        copy.wait()
    for i, out in enumerate((out_a, more_a, out_b, more_b)):
        project_half(info, i, x, i // 2 * 2, w, out)


SMEM, VMEM, ANY = (pl.BlockSpec(memory_space=m) for m in (pltpu.SMEM, pltpu.VMEM, pl.ANY))


def project(kernel, outs, in_specs, scratch, name, *args):
    return pl.pallas_call(
        kernel,
        in_specs=in_specs,
        out_specs=[VMEM] * len(outs),
        out_shape=[jax.ShapeDtypeStruct(shape, BF16) for shape in outs],
        scratch_shapes=scratch,
        compiler_params=params(24),
        cost_estimate=pl.CostEstimate(flops=COST[2], bytes_accessed=2**20, transcendentals=0),
        name=name,
    )(*args)


def pair_sum_kernel(keep, first, out):
    out[...] = (keep[0].astype(F32) + first[0].astype(F32)).astype(BF16)


def pair_sum(keep, first):
    rows = keep.shape[1]
    other = pl.BlockSpec((1, rows, HEAD), lambda i: (1, 0, 0))
    return pl.pallas_call(
        pair_sum_kernel,
        grid=(1,),
        in_specs=[other, other],
        out_specs=pl.BlockSpec((rows, HEAD), lambda i: (0, 0)),
        out_shape=jax.ShapeDtypeStruct((rows, HEAD), BF16),
        compiler_params=params(),
        name="pair_sum",
    )(keep, first)


def finish_kernel(is_key, ka, ra, sa, kb, rb, sb, gain, cos_b, sin_b, cos_i, sin_i, out):
    step = pl.program_id(0)

    def run(keep, first, second):
        total = keep[0].astype(F32) + first[0].astype(F32) + second[...].astype(F32)

        @pl.when(is_key[0] == 0)
        def _():
            out[...] = total.astype(BF16)

        @pl.when(is_key[0] == 1)
        def _():
            scaled = rms_scale(total) * gain[...]
            ci, si = cos_i[...], sin_i[...]
            for b in range(total.shape[0] // BLOCK):
                cb, sb_ = cos_b[b : b + 1, :], sin_b[b : b + 1, :]
                cos = cb * ci - sb_ * si
                sin = sb_ * ci + cb * si
                out[b * BLOCK : (b + 1) * BLOCK, :] = turn(scaled[b * BLOCK : (b + 1) * BLOCK, :], cos, sin).astype(BF16)

    @pl.when(step < 2)
    def _():
        run(ka, ra, sa)

    @pl.when(step >= 2)
    def _():
        run(kb, rb, sb)


def finish(is_key, parts, extra, cost):
    rows = parts[0].shape[1] // 2
    low = lambda i: jnp.minimum(i, 1)
    high = lambda i: jnp.maximum(i - 2, 0)
    specs = []
    for place in (low, high):
        own = pl.BlockSpec((1, rows, HEAD), lambda i, k, place=place: (0, place(i), 0))
        specs += [own, own, pl.BlockSpec((rows, HEAD), lambda i, k, place=place: (place(i), 0))]
    per = pl.BlockSpec((rows // BLOCK, HEAD), lambda i, k: (i, 0))
    whole = lambda a: pl.BlockSpec(a.shape, lambda i, k: (0, 0))
    specs += [whole(extra[0]), per, per, whole(extra[3]), whole(extra[4])]
    return pl.pallas_call(
        finish_kernel,
        grid_spec=pltpu.PrefetchScalarGridSpec(
            num_scalar_prefetch=1,
            grid=(4,),
            in_specs=specs,
            out_specs=pl.BlockSpec((rows, HEAD), lambda i, k: (i, 0)),
        ),
        out_shape=jax.ShapeDtypeStruct((4 * rows, HEAD), BF16),
        compiler_params=params(),
        cost_estimate=pl.CostEstimate(flops=cost, bytes_accessed=2**20, transcendentals=0),
        name="finish",
    )(is_key, *parts, *extra)


def exp_scores(live, line, core, keys, queries):
    scores = lax.dot_general(keys, queries, (((1,), (1,)), ((), ())), preferred_element_type=F32)
    row = lax.broadcasted_iota(jnp.int32, (keys.shape[0], 1), 0)
    limit = jnp.zeros(row.shape, jnp.int32)
    for b in range(keys.shape[0] // BLOCK):
        limit = jnp.where(row >= b * BLOCK, live[line * 8 + 2 * b + core] + b * BLOCK, limit)
    return jnp.where(row < limit, jnp.exp(scores * (1.0 / math.sqrt(HEAD))), 0.0)


def from_core(core):
    return pl.BlockSpec((1, 4, 1, BLOCK, HEAD), lambda i, live: (i, 0, core, 0, 0))


def score_kernel(live, queries, keys, weight, den):
    step = pl.program_id(0)

    @pl.when(step == 0)
    def _():
        den[...] = jnp.zeros_like(den)

    e = exp_scores(live, step, 0, keys[...].reshape(-1, HEAD), queries[...])
    den[...] += jnp.sum(e, axis=0, keepdims=True)
    weight[...] = e.astype(BF16)


def score(live, queries, arrived):
    n = queries.shape[0]
    keys = 4 * BLOCK
    return pl.pallas_call(
        score_kernel,
        grid_spec=pltpu.PrefetchScalarGridSpec(
            num_scalar_prefetch=1,
            grid=(4,),
            in_specs=[pl.BlockSpec((n, HEAD), lambda i, live: (0, 0)), from_core(0)],
            out_specs=(
                pl.BlockSpec((keys, n), lambda i, live: (i, 0)),
                pl.BlockSpec((1, n), lambda i, live: (0, 0)),
            ),
        ),
        out_shape=(jax.ShapeDtypeStruct((4 * keys, n), BF16), jax.ShapeDtypeStruct((1, n), F32)),
        compiler_params=params(),
        cost_estimate=pl.CostEstimate(
            flops=COST[3], bytes_accessed=2**20, transcendentals=0
        ),
        name="score",
    )(live, queries, arrived)


EXTRA = 16


def mix_kernel(live, queries, keys, values, weight, weight_values, den, o0, o1, o2, o3, acc, bottom):
    step = pl.program_id(0)

    e = exp_scores(live, step, 1, keys[...].reshape(-1, HEAD), queries[...])
    here = jnp.sum(e, axis=0, keepdims=True)
    part = 0.0
    for v, w in ((weight_values, weight[...]), (values, e.astype(BF16))):
        flipped = v[...].reshape(-1, HEAD).astype(F32).T.astype(BF16)
        part += lax.dot_general(flipped, w, (((1,), (0,)), ((), ())), preferred_element_type=F32)

    @pl.when(step == 0)
    def _():
        acc[...] = part
        bottom[...] = den[...] + here

    @pl.when(step > 0)
    def _():
        acc[...] += part
        bottom[...] += here

    @pl.when(step == pl.num_programs(0) - 1)
    def _():
        n = o0.shape[1]
        row = lax.broadcasted_iota(jnp.int32, (EXTRA, n), 0)
        for j, out in enumerate((o0, o1, o2, o3)):
            at = pl.ds(pl.multiple_of(((live[32] + j) & 3) * n, n), n)
            out[:HEAD, :] = acc[:, at].astype(BF16)
            d = bottom[:, at]
            coarse = d.astype(BF16).astype(F32)
            tail = jnp.where(row == 0, coarse, jnp.where(row == 1, d - coarse, 0.0))
            out[HEAD:, :] = tail.astype(BF16)


def mix(live, queries, first, second, weight, den):
    total, n = weight.shape
    keys = total // 4
    out = jax.ShapeDtypeStruct((HEAD + EXTRA, n // 4), BF16)
    return pl.pallas_call(
        mix_kernel,
        grid_spec=pltpu.PrefetchScalarGridSpec(
            num_scalar_prefetch=1,
            grid=(4,),
            in_specs=[
                pl.BlockSpec((n, HEAD), lambda i, live: (0, 0)),
                from_core(1),
                from_core(1),
                pl.BlockSpec((keys, n), lambda i, live: (i, 0)),
                from_core(0),
                pl.BlockSpec((1, n), lambda i, live: (0, 0)),
            ],
            out_specs=(pl.BlockSpec(out.shape, lambda i, live: (0, 0)),) * 4,
            scratch_shapes=[pltpu.VMEM((HEAD, n), F32), pltpu.VMEM((1, n), F32)],
        ),
        out_shape=(out,) * 4,
        compiler_params=params(),
        cost_estimate=pl.CostEstimate(
            flops=6 * total * n * HEAD, bytes_accessed=total * n * 2, transcendentals=total * n
        ),
        name="mix",
    )(live, queries, second, first, weight, second, den)


def join_kernel(m0, m1, m2, m3, num, den, out):
    acc = num[...]
    bottom = den[...]
    for m in (m0, m1, m2, m3):
        acc = acc + m[:HEAD, :].astype(F32)
        bottom = bottom + jnp.sum(m[HEAD:, :].astype(F32), axis=0, keepdims=True)
    result = (acc / bottom).T.astype(BF16)
    rows = out.shape[0]
    for head in range(out.shape[1] // HEAD):
        out[:, head * HEAD : (head + 1) * HEAD] = result[head * rows : (head + 1) * rows, :]


def join(messages, num, den, rows):
    n = num.shape[1]
    return pl.pallas_call(
        join_kernel,
        out_shape=jax.ShapeDtypeStruct((rows, n // rows * HEAD), BF16),
        compiler_params=params(),
        name="join",
    )(*messages, num, den)


def on_device(hidden, lengths, owner, w_key, w_value, k_gain, q_gain, dq, dk, dv):
    zh, y, c = lax.axis_index("zh"), lax.axis_index("y"), lax.axis_index("c")
    zl, t = lax.axis_index("zl"), lax.axis_index("x")
    _, prompts, block, width = hidden.shape
    hidden = hidden.reshape(4, prompts // 4 * block, width)
    blocks = 4 * prompts

    w_first = jnp.where(c == 0, w_key, w_value)
    line = [lax.ppermute(w_first, Z_CORE, shift_core(*steps)) for steps in ((1, 1), (-1, -1), (2, -2))]
    delta = jnp.array(DELTA, jnp.int32)
    order = (zh + delta) % 4

    sent = ((t ^ 1, 3 - (t ^ 1)), (3 - t, (3 - t) ^ 1))
    kept = ((t, 3 - t), (t, t ^ 1))

    def info(*pairs):
        heads = jnp.stack([head for pair in pairs for head in pair])
        ahead = (heads - zl) % 4
        place = jnp.where(ahead == 0, 0, jnp.where(ahead == 3, 1, ahead + 1))
        return place.astype(jnp.int32)

    yc = jnp.arange(8, dtype=jnp.int32)
    my_block = ((zh * 8 + y * 2 + c) * 4 + zl).astype(jnp.int32)
    of_group = jnp.arange(4, dtype=jnp.int32)[None, :, None] == order[:, None, None]
    owners = jnp.sum(jnp.where(of_group, owner.reshape(4, 8)[None], 0), axis=1).reshape(-1)
    block_at = (my_block - owners) % blocks
    pick = lambda table, at: jnp.sum(jnp.where(jnp.arange(prompts, dtype=jnp.int32) == at, table, 0))
    my_length = pick(lengths, zh * 8 + y * 2 + c)
    step = jnp.arange(dk.shape[1] * dk.shape[2], dtype=jnp.int32) % dk.shape[2]
    positions = jnp.concatenate([block_at * block, jnp.arange(block, dtype=jnp.int32), my_length + step])
    lane = jnp.arange(HEAD, dtype=jnp.int32)
    frequency = jnp.exp((lane % (HEAD // 2)).astype(F32) * (-2.0 * math.log(1000000.0) / HEAD))
    angles = positions.astype(F32)[:, None] * frequency
    cos = jnp.cos(angles)
    sin = jnp.sin(angles) * jnp.where(lane < HEAD // 2, -1.0, 1.0)
    cut = (prompts, prompts + block)

    rows = dk.shape[1] * dk.shape[2]
    q_mine, num_new, den_new = prep(
        dq.reshape(rows, -1),
        dk.reshape(rows, HEAD),
        dv.reshape(rows, HEAD),
        q_gain[None],
        k_gain[None],
        cos[cut[1] :],
        sin[cut[1] :],
    )

    def join_with(piece, bit):
        other = lax.ppermute(piece, "zl", [(i, i ^ bit) for i in range(4)])
        low = (zl & bit) == 0
        return jnp.concatenate([jnp.where(low, piece, other), jnp.where(low, other, piece)])

    queries = join_with(q_mine, 1)
    queries, cos, sin, *line = lax.optimization_barrier((queries, cos, sin, *line))

    width = w_key.shape[0]
    half_rows = 2 * hidden.shape[1]
    part = (2, half_rows, HEAD)
    tall = (4, width, HEAD)
    four = pltpu.SemaphoreType.DMA((4,))
    send_a, send_b, states, weights = project(
        load_kernel,
        (part, part, hidden.shape, tall),
        [SMEM, pl.BlockSpec(memory_space=pltpu.HBM)] + [ANY] * 4,
        [four, four],
        "project_load",
        jnp.concatenate([info(*sent), order]).astype(jnp.int32),
        hidden,
        w_first,
        *line,
    )
    queries, send_a, send_b = lax.optimization_barrier((queries, send_a, send_b))
    queries = join_with(queries, 2)
    keep_a, keep_b = project(
        more_kernel, (part, part), [SMEM, VMEM, VMEM], [], "project_more", info(*kept), states, weights
    )
    w_key, w_value, send_a, send_b, *line = lax.optimization_barrier((w_key, w_value, send_a, send_b, *line))
    w_second = jnp.where(c == 0, w_value, w_key)
    core = lax.ppermute(jnp.concatenate(line), "c", ((0, 1), (1, 0)))
    next_a, after_a, next_b, after_b = project(
        next_kernel,
        (part,) * 4,
        [SMEM, VMEM] + [ANY] * 4,
        [pltpu.VMEM(tall, BF16), four],
        "project_next",
        info(sent[0], kept[0], sent[1], kept[1]),
        states,
        w_second,
        *(core[i * width : (i + 1) * width] for i in range(3)),
    )
    keep_a, keep_b, next_a, next_b = lax.optimization_barrier((keep_a, keep_b, next_a, next_b))

    in_a = lax.ppermute(send_a, "x", PAIRS[0])
    in_b = lax.ppermute(send_b, "x", PAIRS[1])
    sum_a, sum_b = pair_sum(keep_a, in_a), pair_sum(keep_b, in_b)
    sum_a, sum_b, next_a, next_b = lax.optimization_barrier((sum_a, sum_b, next_a, next_b))
    last_a = lax.ppermute(sum_a, "x", PAIRS[1])
    last_b = lax.ppermute(sum_b, "x", PAIRS[0])
    then_a = lax.ppermute(next_a, "x", PAIRS[0])
    then_b = lax.ppermute(next_b, "x", PAIRS[1])
    then_a, then_b, queries = lax.optimization_barrier((then_a, then_b, queries))
    queries = lax.ppermute(queries, Z_LINE, swap_groups())
    tail_a = lax.ppermute(pair_sum(after_a, then_a), "x", PAIRS[1])
    tail_b = lax.ppermute(pair_sum(after_b, then_b), "x", PAIRS[0])
    tables = (k_gain[None], cos[: cut[0]], sin[: cut[0]], cos[cut[0] : cut[1]], sin[cut[0] : cut[1]])
    second_type = jnp.reshape(c, (1,)).astype(jnp.int32)
    page_first = finish(1 - second_type, (keep_a, in_a, last_a, keep_b, in_b, last_b), tables, COST[0])
    page_second = finish(second_type, (after_a, then_a, tail_a, after_b, then_b, tail_b), tables, COST[1])

    def spread(page):
        page = page.reshape(prompts, block, HEAD)
        got = lax.all_to_all(page, Z_GROUP, split_axis=0, concat_axis=0, tiled=True)
        return got.reshape(4, 4, 2, block, HEAD)

    first = spread(page_first)
    second = spread(page_second)

    group = (zh + jnp.where(zl == 0, 3, jnp.where(zl == 1, 0, jnp.where(zl == 2, 2, 1)))) % 4
    prompt = group * 8 + y * 2 + c
    sources = (zh * 8 + yc[None, :]) * 4 + jnp.arange(4, dtype=jnp.int32)[:, None]
    source_at = (sources.reshape(-1) - pick(owner, prompt)) % blocks
    live = jnp.clip(pick(lengths, prompt) - source_at * block, 0, block)
    live = jnp.concatenate([live, ((zh - group) % 4)[None]]).astype(jnp.int32)
    weight, den = score(live, queries, first)
    messages = mix(live, queries, first, second, weight, den)
    back = [lax.ppermute(m, Z_LINE, route) for m, route in zip(messages, home_routes())]
    out = join(back, num_new, den_new, rows)
    return out.reshape(dq.shape)


def solution(mesh):
    fine = Mesh(mesh.devices.reshape(4, 4, 2, 4, 4), ("zh", "y", "c", "zl", "x"))
    fork = ("zh", "y", "c")
    rows = P(fork, "zl", None, "x")
    in_specs = (
        P(fork, None, "zl", "x"),
        P(),
        P(),
        P("x", "zl"),
        P("x", "zl"),
        P(),
        P(),
        rows,
        rows,
        rows,
    )
    return jax.shard_map(on_device, mesh=fine, in_specs=in_specs, out_specs=rows, check_vma=False)
```

```python
import functools
import math

import jax
import jax.numpy as jnp
from jax import lax
from jax.experimental import pallas as pl
from jax.experimental.pallas import tpu as pltpu
from jax.sharding import Mesh, PartitionSpec as P

BF16 = jnp.bfloat16
F32 = jnp.float32
HEAD = 128
BLOCK = 64
COST = (10**7, 13 * 10**9, 3 * 10**9, 20 * 10**9)
DELTA = (3, 0, 2, 1)
Z_GROUP = ("zl", "y", "c")
Z_LINE = ("zh", "zl")
Z_CORE = ("zh", "c", "zl")
PAIRS = (
    ((0, 1), (1, 0), (2, 3), (3, 2)),
    ((0, 3), (3, 0), (1, 2), (2, 1)),
)


def shift_core(step0, step1):
    place = lambda z, c: (z % 16 // 4 * 2 + c) * 4 + z % 4
    return [(place(z, c), place(z + step, c)) for z in range(16) for c, step in enumerate((step0, step1))]


def home_routes():
    routes = [[] for _ in range(4)]
    for group in range(4):
        for place, delta in enumerate(DELTA):
            prompt_group = (group + delta) % 4
            for rep in range(4):
                routes[(rep + delta) % 4].append((group * 4 + place, prompt_group * 4 + rep))
    return routes


def swap_groups():
    return [(h * 4 + l, (h + d) % 4 * 4 + l ^ m) for h in range(4) for l, (d, m) in enumerate(((3, 3), (0, 0), (2, 0), (1, 3)))]


def params(mib=20):
    return pltpu.CompilerParams(vmem_limit_bytes=mib * 2**20)


def rms_scale(v):
    return v * lax.rsqrt(jnp.mean(v * v, axis=-1, keepdims=True) + 1e-06)


def turn(v, cos, sin):
    return v * cos + pltpu.roll(v, HEAD // 2, 1) * sin


def query_kernel(dq, gain, cos, sin, out):
    rows = dq.shape[0]
    cos, sin = cos[...], sin[...]
    for head in range(dq.shape[1] // HEAD):
        v = dq[:, head * HEAD : (head + 1) * HEAD].astype(F32)
        out[head * rows : (head + 1) * rows, :] = turn(rms_scale(v) * gain[...], cos, sin).astype(BF16)


def turn_queries(dq, gain, cos, sin):
    return pl.pallas_call(
        query_kernel,
        out_shape=jax.ShapeDtypeStruct((dq.size // HEAD, HEAD), BF16),
        compiler_params=params(),
        name="turn_queries",
    )(dq, gain, cos, sin)


def new_kernel(queries, dk, dv, gain, cos, sin, num_out, den_out):
    rows = dk.shape[0]
    key = turn(rms_scale(dk[...].astype(F32)) * gain[...], cos[...], sin[...]).astype(BF16)
    scores = lax.dot_general(key, queries[...], (((1,), (1,)), ((), ())), preferred_element_type=F32)
    k_row = lax.broadcasted_iota(jnp.int32, scores.shape, 0)
    q_col = lax.broadcasted_iota(jnp.int32, scores.shape, 1) & (rows - 1)
    seen = ((k_row >> 3) == (q_col >> 3)) & ((k_row & 7) <= (q_col & 7))
    weight = jnp.where(seen, jnp.exp(scores * (1.0 / math.sqrt(HEAD))), 0.0)
    den_out[...] = jnp.sum(weight, axis=0, keepdims=True)
    num_out[...] = lax.dot_general(
        dv[...].astype(F32).T.astype(BF16), weight.astype(BF16), (((1,), (0,)), ((), ())), preferred_element_type=F32
    )


def new_part(queries, dk, dv, gain, cos, sin):
    n = queries.shape[0]
    return pl.pallas_call(
        new_kernel,
        out_shape=(jax.ShapeDtypeStruct((HEAD, n), F32), jax.ShapeDtypeStruct((1, n), F32)),
        compiler_params=params(),
        name="new_part",
    )(queries, dk, dv, gain, cos, sin)


def project_half(info, i, x, group, w, out):
    both = jnp.concatenate([w[info[2 * i]], w[info[2 * i + 1]]], axis=1)
    n = x.shape[1]
    for k in range(2):
        y = jnp.dot(x[group + k], both, preferred_element_type=F32).astype(BF16)
        out[0, k * n : (k + 1) * n, :] = y[:, :HEAD]
        out[1, k * n : (k + 1) * n, :] = y[:, HEAD:]


def load_kernel(info, hidden, p0, p1, p2, p3, out_a, out_b, x, w, wsem, xsem):
    weights = [pltpu.make_async_copy(p, w.at[j], wsem.at[j]) for j, p in enumerate((p0, p1, p2, p3))]
    states = [pltpu.make_async_copy(hidden.at[info[4 + i]], x.at[i], xsem.at[i]) for i in range(4)]
    for copy in weights + states:
        copy.start()
    for copy in weights:
        copy.wait()
    for half, out in enumerate((out_a, out_b)):
        for copy in states[2 * half : 2 * half + 2]:
            copy.wait()
        project_half(info, half, x, 2 * half, w, out)


def more_kernel(info, x, w, out_a, out_b):
    for half, out in enumerate((out_a, out_b)):
        project_half(info, half, x, 2 * half, w, out)


def next_kernel(info, x, p0, p1, p2, p3, out_a, more_a, out_b, more_b, w, wsem):
    weights = [pltpu.make_async_copy(p, w.at[j], wsem.at[j]) for j, p in enumerate((p0, p1, p2, p3))]
    for copy in weights:
        copy.start()
    for copy in weights:
        copy.wait()
    for i, out in enumerate((out_a, more_a, out_b, more_b)):
        project_half(info, i, x, i // 2 * 2, w, out)


SMEM, VMEM, ANY = (pl.BlockSpec(memory_space=m) for m in (pltpu.SMEM, pltpu.VMEM, pl.ANY))


def project(kernel, outs, in_specs, scratch, name, *args):
    return pl.pallas_call(
        kernel,
        in_specs=in_specs,
        out_specs=[VMEM] * len(outs),
        out_shape=[jax.ShapeDtypeStruct(shape, BF16) for shape in outs],
        scratch_shapes=scratch,
        compiler_params=params(24),
        cost_estimate=pl.CostEstimate(flops=COST[2], bytes_accessed=2**20, transcendentals=0),
        name=name,
    )(*args)


def pair_sum_kernel(keep, first, out):
    out[...] = (keep[0].astype(F32) + first[0].astype(F32)).astype(BF16)


def pair_sum(keep, first):
    rows = keep.shape[1]
    other = pl.BlockSpec((1, rows, HEAD), lambda i: (1, 0, 0))
    return pl.pallas_call(
        pair_sum_kernel,
        grid=(1,),
        in_specs=[other, other],
        out_specs=pl.BlockSpec((rows, HEAD), lambda i: (0, 0)),
        out_shape=jax.ShapeDtypeStruct((rows, HEAD), BF16),
        compiler_params=params(),
        name="pair_sum",
    )(keep, first)


def finish_kernel(is_key, ka, ra, sa, kb, rb, sb, gain, cos_b, sin_b, cos_i, sin_i, out):
    step = pl.program_id(0)

    def run(keep, first, second):
        total = keep[0].astype(F32) + first[0].astype(F32) + second[...].astype(F32)

        @pl.when(is_key[0] == 0)
        def _():
            out[...] = total.astype(BF16)

        @pl.when(is_key[0] == 1)
        def _():
            scaled = rms_scale(total) * gain[...]
            ci, si = cos_i[...], sin_i[...]
            for b in range(total.shape[0] // BLOCK):
                cb, sb_ = cos_b[b : b + 1, :], sin_b[b : b + 1, :]
                cos = cb * ci - sb_ * si
                sin = sb_ * ci + cb * si
                out[b * BLOCK : (b + 1) * BLOCK, :] = turn(scaled[b * BLOCK : (b + 1) * BLOCK, :], cos, sin).astype(BF16)

    @pl.when(step < 2)
    def _():
        run(ka, ra, sa)

    @pl.when(step >= 2)
    def _():
        run(kb, rb, sb)


def finish(is_key, parts, extra, cost):
    rows = parts[0].shape[1] // 2
    low = lambda i: jnp.minimum(i, 1)
    high = lambda i: jnp.maximum(i - 2, 0)
    specs = []
    for place in (low, high):
        own = pl.BlockSpec((1, rows, HEAD), lambda i, k, place=place: (0, place(i), 0))
        specs += [own, own, pl.BlockSpec((rows, HEAD), lambda i, k, place=place: (place(i), 0))]
    per = pl.BlockSpec((rows // BLOCK, HEAD), lambda i, k: (i, 0))
    whole = lambda a: pl.BlockSpec(a.shape, lambda i, k: (0, 0))
    specs += [whole(extra[0]), per, per, whole(extra[3]), whole(extra[4])]
    return pl.pallas_call(
        finish_kernel,
        grid_spec=pltpu.PrefetchScalarGridSpec(
            num_scalar_prefetch=1,
            grid=(4,),
            in_specs=specs,
            out_specs=pl.BlockSpec((rows, HEAD), lambda i, k: (i, 0)),
        ),
        out_shape=jax.ShapeDtypeStruct((4 * rows, HEAD), BF16),
        compiler_params=params(),
        cost_estimate=pl.CostEstimate(flops=cost, bytes_accessed=2**20, transcendentals=0),
        name="finish",
    )(is_key, *parts, *extra)


def exp_scores(live, line, core, keys, queries):
    scores = lax.dot_general(keys, queries, (((1,), (1,)), ((), ())), preferred_element_type=F32)
    row = lax.broadcasted_iota(jnp.int32, (keys.shape[0], 1), 0)
    limit = jnp.zeros(row.shape, jnp.int32)
    for b in range(keys.shape[0] // BLOCK):
        limit = jnp.where(row >= b * BLOCK, live[line * 8 + 2 * b + core] + b * BLOCK, limit)
    return jnp.where(row < limit, jnp.exp(scores * (1.0 / math.sqrt(HEAD))), 0.0)


def from_core(core):
    return pl.BlockSpec((1, 4, 1, BLOCK, HEAD), lambda i, live: (i, 0, core, 0, 0))


def score_kernel(live, queries, keys, weight, den):
    step = pl.program_id(0)

    @pl.when(step == 0)
    def _():
        den[...] = jnp.zeros_like(den)

    e = exp_scores(live, step, 0, keys[...].reshape(-1, HEAD), queries[...])
    den[...] += jnp.sum(e, axis=0, keepdims=True)
    weight[...] = e.astype(BF16)


def score(live, queries, arrived):
    n = queries.shape[0]
    keys = 4 * BLOCK
    return pl.pallas_call(
        score_kernel,
        grid_spec=pltpu.PrefetchScalarGridSpec(
            num_scalar_prefetch=1,
            grid=(4,),
            in_specs=[pl.BlockSpec((n, HEAD), lambda i, live: (0, 0)), from_core(0)],
            out_specs=(
                pl.BlockSpec((keys, n), lambda i, live: (i, 0)),
                pl.BlockSpec((1, n), lambda i, live: (0, 0)),
            ),
        ),
        out_shape=(jax.ShapeDtypeStruct((4 * keys, n), BF16), jax.ShapeDtypeStruct((1, n), F32)),
        compiler_params=params(),
        cost_estimate=pl.CostEstimate(
            flops=COST[3], bytes_accessed=2**20, transcendentals=0
        ),
        name="score",
    )(live, queries, arrived)


EXTRA = 16


def mix_kernel(live, queries, keys, values, weight, weight_values, den, o0, o1, o2, o3, acc, bottom):
    step = pl.program_id(0)

    e = exp_scores(live, step, 1, keys[...].reshape(-1, HEAD), queries[...])
    here = jnp.sum(e, axis=0, keepdims=True)
    part = 0.0
    for v, w in ((weight_values, weight[...]), (values, e.astype(BF16))):
        flipped = v[...].reshape(-1, HEAD).astype(F32).T.astype(BF16)
        part += lax.dot_general(flipped, w, (((1,), (0,)), ((), ())), preferred_element_type=F32)

    @pl.when(step == 0)
    def _():
        acc[...] = part
        bottom[...] = den[...] + here

    @pl.when(step > 0)
    def _():
        acc[...] += part
        bottom[...] += here

    @pl.when(step == pl.num_programs(0) - 1)
    def _():
        n = o0.shape[1]
        row = lax.broadcasted_iota(jnp.int32, (EXTRA, n), 0)
        for j, out in enumerate((o0, o1, o2, o3)):
            at = pl.ds(pl.multiple_of(((live[32] + j) & 3) * n, n), n)
            out[:HEAD, :] = acc[:, at].astype(BF16)
            d = bottom[:, at]
            coarse = d.astype(BF16).astype(F32)
            tail = jnp.where(row == 0, coarse, jnp.where(row == 1, d - coarse, 0.0))
            out[HEAD:, :] = tail.astype(BF16)


def mix(live, queries, first, second, weight, den):
    total, n = weight.shape
    keys = total // 4
    out = jax.ShapeDtypeStruct((HEAD + EXTRA, n // 4), BF16)
    return pl.pallas_call(
        mix_kernel,
        grid_spec=pltpu.PrefetchScalarGridSpec(
            num_scalar_prefetch=1,
            grid=(4,),
            in_specs=[
                pl.BlockSpec((n, HEAD), lambda i, live: (0, 0)),
                from_core(1),
                from_core(1),
                pl.BlockSpec((keys, n), lambda i, live: (i, 0)),
                from_core(0),
                pl.BlockSpec((1, n), lambda i, live: (0, 0)),
            ],
            out_specs=(pl.BlockSpec(out.shape, lambda i, live: (0, 0)),) * 4,
            scratch_shapes=[pltpu.VMEM((HEAD, n), F32), pltpu.VMEM((1, n), F32)],
        ),
        out_shape=(out,) * 4,
        compiler_params=params(),
        cost_estimate=pl.CostEstimate(
            flops=6 * total * n * HEAD, bytes_accessed=total * n * 2, transcendentals=total * n
        ),
        name="mix",
    )(live, queries, second, first, weight, second, den)


def join_kernel(m0, m1, m2, m3, num, den, out):
    acc = num[...]
    bottom = den[...]
    for m in (m0, m1, m2, m3):
        acc = acc + m[:HEAD, :].astype(F32)
        bottom = bottom + jnp.sum(m[HEAD:, :].astype(F32), axis=0, keepdims=True)
    result = (acc / bottom).T.astype(BF16)
    rows = out.shape[0]
    for head in range(out.shape[1] // HEAD):
        out[:, head * HEAD : (head + 1) * HEAD] = result[head * rows : (head + 1) * rows, :]


def join(messages, num, den, rows):
    n = num.shape[1]
    return pl.pallas_call(
        join_kernel,
        out_shape=jax.ShapeDtypeStruct((rows, n // rows * HEAD), BF16),
        compiler_params=params(),
        name="join",
    )(*messages, num, den)


def on_device(hidden, lengths, owner, w_key, w_value, k_gain, q_gain, dq, dk, dv):
    zh, y, c = lax.axis_index("zh"), lax.axis_index("y"), lax.axis_index("c")
    zl, t = lax.axis_index("zl"), lax.axis_index("x")
    _, prompts, block, width = hidden.shape
    hidden = hidden.reshape(4, prompts // 4 * block, width)
    blocks = 4 * prompts

    w_first = jnp.where(c == 0, w_key, w_value)
    line = [lax.ppermute(w_first, Z_CORE, shift_core(*steps)) for steps in ((1, 1), (-1, -1), (2, -2))]
    delta = jnp.array(DELTA, jnp.int32)
    order = (zh + delta) % 4

    sent = ((t ^ 1, 3 - (t ^ 1)), (3 - t, (3 - t) ^ 1))
    kept = ((t, 3 - t), (t, t ^ 1))

    def info(*pairs):
        heads = jnp.stack([head for pair in pairs for head in pair])
        ahead = (heads - zl) % 4
        place = jnp.where(ahead == 0, 0, jnp.where(ahead == 3, 1, ahead + 1))
        return place.astype(jnp.int32)

    yc = jnp.arange(8, dtype=jnp.int32)
    my_block = ((zh * 8 + y * 2 + c) * 4 + zl).astype(jnp.int32)
    of_group = jnp.arange(4, dtype=jnp.int32)[None, :, None] == order[:, None, None]
    owners = jnp.sum(jnp.where(of_group, owner.reshape(4, 8)[None], 0), axis=1).reshape(-1)
    block_at = (my_block - owners) % blocks
    pick = lambda table, at: jnp.sum(jnp.where(jnp.arange(prompts, dtype=jnp.int32) == at, table, 0))
    my_length = pick(lengths, zh * 8 + y * 2 + c)
    step = jnp.arange(dk.shape[1] * dk.shape[2], dtype=jnp.int32) % dk.shape[2]
    positions = jnp.concatenate([block_at * block, jnp.arange(block, dtype=jnp.int32), my_length + step])
    lane = jnp.arange(HEAD, dtype=jnp.int32)
    frequency = jnp.exp((lane % (HEAD // 2)).astype(F32) * (-2.0 * math.log(1000000.0) / HEAD))
    angles = positions.astype(F32)[:, None] * frequency
    cos = jnp.cos(angles)
    sin = jnp.sin(angles) * jnp.where(lane < HEAD // 2, -1.0, 1.0)
    cut = (prompts, prompts + block)

    rows = dk.shape[1] * dk.shape[2]
    q_mine = turn_queries(dq.reshape(rows, -1), q_gain[None], cos[cut[1] :], sin[cut[1] :])

    def join_with(piece, bit):
        other = lax.ppermute(piece, "zl", [(i, i ^ bit) for i in range(4)])
        low = (zl & bit) == 0
        return jnp.concatenate([jnp.where(low, piece, other), jnp.where(low, other, piece)])

    queries = join_with(q_mine, 1)
    queries, cos, sin, *line = lax.optimization_barrier((queries, cos, sin, *line))

    width = w_key.shape[0]
    half_rows = 2 * hidden.shape[1]
    part = (2, half_rows, HEAD)
    tall = (4, width, HEAD)
    four = pltpu.SemaphoreType.DMA((4,))
    send_a, send_b, states, weights = project(
        load_kernel,
        (part, part, hidden.shape, tall),
        [SMEM, pl.BlockSpec(memory_space=pltpu.HBM)] + [ANY] * 4,
        [four, four],
        "project_load",
        jnp.concatenate([info(*sent), order]).astype(jnp.int32),
        hidden,
        w_first,
        *line,
    )
    queries, send_a, send_b = lax.optimization_barrier((queries, send_a, send_b))
    queries = join_with(queries, 2)
    keep_a, keep_b = project(
        more_kernel, (part, part), [SMEM, VMEM, VMEM], [], "project_more", info(*kept), states, weights
    )
    w_key, w_value, send_a, send_b, *line = lax.optimization_barrier((w_key, w_value, send_a, send_b, *line))
    w_second = jnp.where(c == 0, w_value, w_key)
    core = lax.ppermute(jnp.concatenate(line), "c", ((0, 1), (1, 0)))
    next_a, after_a, next_b, after_b = project(
        next_kernel,
        (part,) * 4,
        [SMEM, VMEM] + [ANY] * 4,
        [pltpu.VMEM(tall, BF16), four],
        "project_next",
        info(sent[0], kept[0], sent[1], kept[1]),
        states,
        w_second,
        *(core[i * width : (i + 1) * width] for i in range(3)),
    )
    keep_a, keep_b, next_a, next_b = lax.optimization_barrier((keep_a, keep_b, next_a, next_b))

    in_a = lax.ppermute(send_a, "x", PAIRS[0])
    in_b = lax.ppermute(send_b, "x", PAIRS[1])
    sum_a, sum_b = pair_sum(keep_a, in_a), pair_sum(keep_b, in_b)
    sum_a, sum_b, next_a, next_b, queries = lax.optimization_barrier((sum_a, sum_b, next_a, next_b, queries))
    last_a = lax.ppermute(sum_a, "x", PAIRS[1])
    last_b = lax.ppermute(sum_b, "x", PAIRS[0])
    then_a = lax.ppermute(next_a, "x", PAIRS[0])
    then_b = lax.ppermute(next_b, "x", PAIRS[1])
    then_a, then_b, queries = lax.optimization_barrier((then_a, then_b, queries))
    queries = lax.ppermute(queries, Z_LINE, swap_groups())
    tail_a = lax.ppermute(pair_sum(after_a, then_a), "x", PAIRS[1])
    tail_b = lax.ppermute(pair_sum(after_b, then_b), "x", PAIRS[0])
    tables = (k_gain[None], cos[: cut[0]], sin[: cut[0]], cos[cut[0] : cut[1]], sin[cut[0] : cut[1]])
    second_type = jnp.reshape(c, (1,)).astype(jnp.int32)
    page_first = finish(1 - second_type, (keep_a, in_a, last_a, keep_b, in_b, last_b), tables, COST[0])
    page_second = finish(second_type, (after_a, then_a, tail_a, after_b, then_b, tail_b), tables, COST[1])

    def spread(page):
        page = page.reshape(prompts, block, HEAD)
        got = lax.all_to_all(page, Z_GROUP, split_axis=0, concat_axis=0, tiled=True)
        return got.reshape(4, 4, 2, block, HEAD)

    first = spread(page_first)
    second = spread(page_second)

    group = (zh + jnp.where(zl == 0, 3, jnp.where(zl == 1, 0, jnp.where(zl == 2, 2, 1)))) % 4
    prompt = group * 8 + y * 2 + c
    sources = (zh * 8 + yc[None, :]) * 4 + jnp.arange(4, dtype=jnp.int32)[:, None]
    source_at = (sources.reshape(-1) - pick(owner, prompt)) % blocks
    live = jnp.clip(pick(lengths, prompt) - source_at * block, 0, block)
    live = jnp.concatenate([live, ((zh - group) % 4)[None]]).astype(jnp.int32)
    weight, den = score(live, queries, first)
    messages = mix(live, queries, first, second, weight, den)
    back = [lax.ppermute(m, Z_LINE, route) for m, route in zip(messages, home_routes())]
    num_new, den_new = new_part(
        q_mine, dk.reshape(rows, HEAD), dv.reshape(rows, HEAD), k_gain[None], cos[cut[1] :], sin[cut[1] :]
    )
    out = join(back, num_new, den_new, rows)
    return out.reshape(dq.shape)


def solution(mesh):
    fine = Mesh(mesh.devices.reshape(4, 4, 2, 4, 4), ("zh", "y", "c", "zl", "x"))
    fork = ("zh", "y", "c")
    rows = P(fork, "zl", None, "x")
    in_specs = (
        P(fork, None, "zl", "x"),
        P(),
        P(),
        P("x", "zl"),
        P("x", "zl"),
        P(),
        P(),
        rows,
        rows,
        rows,
    )
    return jax.shard_map(on_device, mesh=fine, in_specs=in_specs, out_specs=rows, check_vma=False)
```
